256 devices in a mesh: dp: 64 (over z, y, core), mp: 4 (over x).
Axes of the slice: x: 4, y: 4, z: 8, core: 2. Of those that a mesh axis runs over, the one named last changes fastest.
Arguments:
- query: bfloat16 [16384, 3072], P('dp', 'mp'), may hold values from -6 to 6
- key: bfloat16 [16384, 3072], P('dp', 'mp'), may hold values from -6 to 6
- value: bfloat16 [16384, 3072], P('dp', 'mp'), may hold values from -6 to 6
- send_to: int32 [16384], P('dp'), may hold values from 0 to 63, as said below
- recv_from: int32 [16384], P('dp'), may hold values from 0 to 63, as said below
- segment: int32 [16384], P('dp'), may hold values from 0 to 15, as said below
- out_weight: bfloat16 [3072, 3072], P('dp', 'mp'), may hold values from -0.109375 to 0.109375
- cotangent: bfloat16 [16384, 3072], P('dp', 'mp'), may hold values from -16 to 16
Outputs:
- grad_query: bfloat16 [16384, 3072], P('dp', 'mp')
- grad_key: bfloat16 [16384, 3072], P('dp', 'mp')
- grad_value: bfloat16 [16384, 3072], P('dp', 'mp')
- update: float32 [3072, 3072], P('dp', 'mp')
The draws below stay inside these ranges and needn't reach their ends.
Inputs may be any that keep to these rules, and one draw needn't show every extreme that they name: `send_to`: the rows of one loader shard are grouped by destination in increasing order; at most 6 rows of one loader shard go to one sequence, and exactly 6 in some pair. `recv_from`: the positions of one sequence are grouped by source shard in increasing order; sequence d takes from shard s exactly as many positions as shard s has rows naming d. `segment`: within one sequence image ids start at 0 and never fall; some sequence reaches the largest id.
All inputs are finite; a program needn't handle non-finite values.
Results may differ from the reference program's by a relative error of at most 0.013.
Values may be sent and summed in bfloat16 or wider, within the bound.
No kernel may reach another device: no remote copies, remote signals or barrier semaphores. Data moves between devices by JAX's collectives and lax.ppermute only.
A program may use at most 128 MiB of HBM per device.

```python
import math
import jax
import jax.numpy as jnp
from jax import lax

D = 3072
HEADS = 24
HD = 128
ROWS = 256
NS_STEPS = 3
INNER = 3072
TOKENS = 16384
N_DP = 64


def paired_fields(key):
    base_q = jnp.clip(jax.random.normal(jax.random.fold_in(key, 21), (TOKENS, INNER), jnp.float32), -6.0, 6.0)
    base_k = jnp.clip(jax.random.normal(jax.random.fold_in(key, 22), (TOKENS, INNER), jnp.float32), -6.0, 6.0)
    q_out = base_q
    k_out = base_k
    return (q_out, k_out)


def draw_query(key, part):
    return paired_fields(key)[0].astype(jnp.bfloat16)


def draw_key(key, part):
    return paired_fields(key)[1].astype(jnp.bfloat16)


def routing_plan(key):
    order_a = jax.random.permutation(jax.random.fold_in(key, 101), N_DP).astype(jnp.int32)
    order_b = jax.random.permutation(jax.random.fold_in(key, 102), N_DP).astype(jnp.int32)
    span = N_DP // 8
    index = jnp.arange(N_DP, dtype=jnp.int32)
    pattern = jnp.where(index < span, 2, jnp.where(index < 2 * span, -2, jnp.where(index < 3 * span, 1, jnp.where(index < 4 * span, -1, 0)))).astype(jnp.int32)
    counts = ROWS // N_DP + pattern[(order_a[None, :] + order_b[:, None]) % N_DP]
    position = jnp.arange(ROWS, dtype=jnp.int32)
    send_cum = jnp.cumsum(counts, axis=1)
    send_plan = jnp.sum((position[None, :, None] >= send_cum[:, None, :]).astype(jnp.int32), axis=2)
    recv_cum = jnp.cumsum(counts, axis=0).T
    recv_plan = jnp.sum((position[None, :, None] >= recv_cum[:, None, :]).astype(jnp.int32), axis=2)
    return (send_plan.reshape(-1).astype(jnp.int32), recv_plan.reshape(-1).astype(jnp.int32))


def draw_send_to(key, part):
    return routing_plan(key)[0]


def draw_recv_from(key, part):
    return routing_plan(key)[1]


def draw_segment(key, part):
    key = jax.random.fold_in(key, 5)
    flags = (jax.random.randint(key, (N_DP, ROWS), 0, 24) == 0).astype(jnp.int32)
    chosen = jax.random.randint(jax.random.fold_in(key, 6), (), 0, N_DP)
    position = jnp.arange(ROWS, dtype=jnp.int32)
    regular = (position % 16 == 0).astype(jnp.int32)
    is_chosen = (jnp.arange(N_DP, dtype=jnp.int32) == chosen)[:, None]
    flags = jnp.where(is_chosen, regular[None, :], flags)
    flags = flags.at[:, 0].set(0)
    ids = jnp.minimum(jnp.cumsum(flags, axis=1), ROWS // 16 - 1)
    return ids.reshape(-1).astype(jnp.int32)


def with_spikes(values, stream_key, source, target, parts, factor):
    owner, partner = [(jnp.arange(values.shape[dim]) // (values.shape[dim] // parts)).reshape([-1 if axis == dim else 1 for axis in range(values.ndim)]) for dim in (source, target)]
    chosen = jax.random.permutation(stream_key, parts)[partner]
    strong = (owner == chosen) | (owner == (partner + parts // 2) % parts)
    return jnp.where(strong, factor * values, values)


def block_scale(stream_key, dims, cuts, smallest, top_value):
    level, own = 1.0, jax.random.fold_in(stream_key, 6)
    for dim, blocks in cuts:
        steps = jnp.exp(jax.random.uniform(jax.random.fold_in(own, dim), (blocks,), jnp.float32, smallest / len(cuts), top_value / len(cuts)))
        level = level * jnp.repeat(steps, dims[dim] // blocks).reshape([-1 if axis == dim else 1 for axis in range(len(dims))])
    return level


def scatter_about(rng, shape, scale, limit, shards=(), kind=jnp.bfloat16):
    values = scale * jax.random.normal(rng, shape, jnp.float32)
    if shards:
        values = values * block_scale(rng, shape, shards, -0.22, 0.18)
    return jnp.clip(values, -limit, limit).astype(kind)


def noise_with(key, shape, spread, most, pieces, heavy, held_as=jnp.bfloat16):
    values = spread * jax.random.normal(key, shape, jnp.float32)
    if pieces:
        values = values * block_scale(key, shape, pieces, -0.22, 0.18)
    return jnp.clip(with_spikes(values, jax.random.fold_in(key, 3), *heavy), -most, most).astype(held_as)


def setup_inputs(seed: int = 0) -> dict:
    splits = jax.random.split(jax.random.key(seed), 9)
    query = draw_query(jax.random.fold_in(splits[8], 71), 0)
    key = draw_key(jax.random.fold_in(splits[8], 71), 0)
    value = scatter_about(splits[2], (TOKENS, INNER), 1.0, 6.0, ((0, 64), (1, 4)))
    send_to = draw_send_to(jax.random.fold_in(splits[8], 71), 0)
    recv_from = draw_recv_from(jax.random.fold_in(splits[8], 71), 0)
    segment = draw_segment(jax.random.fold_in(splits[8], 71), 0)
    out_weight = scatter_about(splits[6], (D, INNER), D ** -0.5, 0.109375, ((0, 64), (1, 4)))
    cotangent = noise_with(splits[7], (TOKENS, D), 1.0, 16.0, ((0, 64), (1, 4)), (0, 1, 64, 4.0))
    return dict(query=query, key=key, value=value, send_to=send_to, recv_from=recv_from, segment=segment, out_weight=out_weight, cotangent=cotangent)


coef_a = 3.4445
coef_b = -4.775
coef_c = 2.0315
norm_eps = 1e-07

def repack_index(send_to, recv_from):
    send_grid = send_to.reshape(N_DP, ROWS)
    recv_grid = recv_from.reshape(N_DP, ROWS)
    peers = jnp.arange(N_DP, dtype=jnp.int32)
    sent_count = lax.optimization_barrier(jnp.sum((send_grid[:, :, None] == peers[None, None, :]).astype(jnp.int32), axis=1))
    sent_start = jnp.cumsum(sent_count, axis=1) - sent_count
    recv_count = lax.optimization_barrier(jnp.sum((recv_grid[:, :, None] == peers[None, None, :]).astype(jnp.int32), axis=1))
    recv_start = jnp.cumsum(recv_count, axis=1) - recv_count
    dest_grid = jnp.broadcast_to(peers[:, None], (N_DP, ROWS))
    position = jnp.broadcast_to(jnp.arange(ROWS, dtype=jnp.int32)[None, :], (N_DP, ROWS))
    rank = position - recv_start[dest_grid, recv_grid]
    source_row = recv_grid * ROWS + sent_start[recv_grid, dest_grid] + rank
    return source_row.reshape(-1).astype(jnp.int32)

def one_sequence(items):
    q_rows, k_rows, v_rows, seg_rows, cot_rows, weight = items
    scale = 1.0 / math.sqrt(HD)
    qh = q_rows.reshape(ROWS, HEADS, HD).astype(jnp.float32)
    kh = k_rows.reshape(ROWS, HEADS, HD).astype(jnp.float32)
    vh = v_rows.reshape(ROWS, HEADS, HD).astype(jnp.float32)
    scores = jnp.einsum('qhd,khd->hqk', qh, kh) * scale
    same = seg_rows[:, None] == seg_rows[None, :]
    scores = jnp.where(same[None, :, :], scores, -jnp.inf)
    top = lax.optimization_barrier(jnp.max(scores, axis=-1, keepdims=True))
    expo = jnp.exp(scores - top)
    prob_float = expo / lax.optimization_barrier(jnp.sum(expo, axis=-1, keepdims=True))
    prob = prob_float.astype(jnp.bfloat16)
    attended = jnp.einsum('hqk,khd->qhd', prob.astype(jnp.float32), vh).astype(jnp.bfloat16)
    d_attended = jnp.dot(cot_rows, weight, preferred_element_type=jnp.float32).astype(jnp.bfloat16)
    d_out = d_attended.reshape(ROWS, HEADS, HD).astype(jnp.float32)
    grad_value = jnp.einsum('hqk,qhd->khd', prob.astype(jnp.float32), d_out).astype(jnp.bfloat16)
    d_prob = jnp.einsum('qhd,khd->hqk', d_out, vh)
    delta = lax.optimization_barrier(jnp.sum(d_prob * prob_float, axis=-1, keepdims=True))
    d_score = (prob_float * (d_prob - delta) * scale).astype(jnp.bfloat16).astype(jnp.float32)
    grad_query = jnp.einsum('hqk,khd->qhd', d_score, kh).astype(jnp.bfloat16)
    grad_key = jnp.einsum('hqk,qhd->khd', d_score, qh).astype(jnp.bfloat16)
    return (grad_query.reshape(ROWS, INNER), grad_key.reshape(ROWS, INNER), grad_value.reshape(ROWS, INNER), attended.reshape(ROWS, INNER))

def newton_schulz(grad3):
    norm = jnp.sqrt(lax.optimization_barrier(jnp.sum(grad3 * grad3, axis=(0, 2))))
    current = grad3 / (norm[None, :, None] + norm_eps)
    high = lax.Precision.HIGHEST
    for iteration in range(NS_STEPS):
        gram = jnp.einsum('dhi,dhj->hij', current, current, precision=high)
        square = jnp.einsum('hij,hjk->hik', gram, gram, precision=high)
        mixer = coef_b * gram + coef_c * square
        current = coef_a * current + jnp.einsum('dhi,hij->dhj', current, mixer, precision=high)
    return current

def reference(query, key, value, send_to, recv_from, segment, out_weight, cotangent):
    source_row = repack_index(send_to, recv_from)
    packed_q = query[source_row].reshape(N_DP, ROWS, INNER)
    packed_k = key[source_row].reshape(N_DP, ROWS, INNER)
    packed_v = value[source_row].reshape(N_DP, ROWS, INNER)
    seg_grid = segment.reshape(N_DP, ROWS)
    cot_grid = cotangent.reshape(N_DP, ROWS, D)

    def run(items):
        return one_sequence(items + (out_weight,))
    grad_query, grad_key, grad_value, attended = lax.map(run, (packed_q, packed_k, packed_v, seg_grid, cot_grid))
    attended_all = attended.reshape(TOKENS, INNER)
    weight_grad = jnp.dot(cotangent.T, attended_all, preferred_element_type=jnp.float32)
    result = newton_schulz(weight_grad.reshape(D, HEADS, HD))
    update = (math.sqrt(D) * result).reshape(D, INNER)
    return (grad_query.reshape(TOKENS, INNER), grad_key.reshape(TOKENS, INNER), grad_value.reshape(TOKENS, INNER), update)
```

```python
import math

import jax
import jax.numpy as jnp
from jax import lax
from jax.experimental import pallas as pl
from jax.experimental.pallas import tpu as pltpu
from jax.sharding import Mesh, PartitionSpec as P

D = 3072
HD = 128
ROWS = 256
GROUPS = 64
SLOTS = 6
HEADS_HERE = 6
BLOCKS = 3 * HEADS_HERE
TILE = 16
TILES = 7
FLAT = GROUPS * TILE
Z, Y, C, X = 8, 4, 2, 4
FEAT = 48
HALF = HEADS_HERE * HD // 2
NS_STEPS = 3

coef_a = 3.4445
coef_b = -4.775
coef_c = 2.0315
norm_eps = 1e-07
scale = 1.0 / math.sqrt(HD)
f32 = jnp.float32
bf16 = jnp.bfloat16


def find_patterns():
    found = []
    for tile in range(3):
        rows = [tile * TILE + i for i in range(TILE)]
        for block in sorted({r // SLOTS for r in rows}):
            found.append((tile, block))
    return found


PATTERNS = find_patterns()


def pattern_users(tile, block):
    return [
        (tile + 3 * n, block + 8 * n)
        for n in range(3)
        if tile + 3 * n < TILES and block + 8 * n < BLOCKS
    ]


def place_kernel(label_ref, q_hbm, k_hbm, v_hbm, out_ref, q_ref, k_ref, v_ref, sems):
    fields = (q_ref, k_ref, v_ref)
    copies = [
        pltpu.make_async_copy(source, target, sems.at[n])
        for n, (source, target) in enumerate(zip((q_hbm, k_hbm, v_hbm), fields))
    ]
    for copy in copies:
        copy.start()

    label = label_ref[...]
    group = lax.broadcasted_iota(jnp.int32, (GROUPS, ROWS), 0)
    before = jnp.sum(jnp.where(label < group, 1, 0), axis=1, keepdims=True)
    start = jnp.sum(jnp.where(label == group, before, 0), axis=0, keepdims=True)
    code = 8 * label + lax.broadcasted_iota(jnp.int32, (1, ROWS), 1) - start

    def block_of(j):
        return fields[j // HEADS_HERE][:, (j % HEADS_HERE) * HD : (j % HEADS_HERE + 1) * HD]

    row = lax.broadcasted_iota(jnp.int32, (TILE, ROWS), 0)
    eights = 8 * lax.broadcasted_iota(jnp.int32, (GROUPS, TILE, ROWS), 0)
    for copy in copies:
        copy.wait()
    for first in range(3):
        total = {}
        for tile, block in PATTERNS:
            if tile != first:
                continue
            slot = row + (TILE * tile - SLOTS * block)
            wanted = jnp.where((slot >= 0) & (slot < SLOTS), code - slot, -1)
            hot = jnp.where(eights == wanted[None], 1.0, 0.0).astype(bf16).reshape(FLAT, ROWS)
            users = pattern_users(tile, block)
            wide = jnp.concatenate([block_of(j) for _, j in users], axis=1)
            got = jnp.dot(hot, wide, preferred_element_type=f32)
            for n, (t, _) in enumerate(users):
                part = got[:, n * HD : (n + 1) * HD]
                total[t] = part if t not in total else total[t] + part
        for t, rows in total.items():
            out_ref[:, t * TILE : (t + 1) * TILE, :] = rows.astype(bf16).reshape(GROUPS, TILE, HD)


def parts_kernel(cot_ref, weight_ref, *out_refs):
    weight = weight_ref[...]
    for k, out_ref in enumerate(out_refs):
        out_ref[...] = lax.dot_general(
            cot_ref[k], weight, (((0,), (0,)), ((), ())), preferred_element_type=f32
        ).astype(bf16)


def soft(q, k, same):
    scores = (
        lax.dot_general(q, k, (((1,), (1,)), ((), ())), preferred_element_type=f32) * scale
    )
    scores = jnp.where(same, scores, -jnp.inf)
    top = jnp.max(scores, axis=-1, keepdims=True)
    expo = jnp.exp(scores - top)
    return expo / jnp.sum(expo, axis=-1, keepdims=True)


def forward_kernel(
    core_ref, from_row, from_col, row_ref, col_ref, slots_ref, packed_ref, own_ref, other_ref
):
    before = jnp.sum(jnp.where(from_row[...] < from_col[...], 1, 0), axis=1, keepdims=True)
    code = 8 * from_col[...] + lax.broadcasted_iota(jnp.int32, (ROWS, 1), 0) - before
    lane = lax.broadcasted_iota(jnp.int32, (1, FLAT), 1)
    group = lane // TILE
    total = {}
    for tile, block in PATTERNS:
        slot = lane - TILE * group + (TILE * tile - SLOTS * block)
        wanted = jnp.where((slot >= 0) & (slot < SLOTS), 8 * group + slot, -1)
        hot = jnp.where(code == wanted, 1.0, 0.0).astype(bf16)
        users = pattern_users(tile, block)
        wide = jnp.concatenate(
            [
                slots_ref[:, t * TILE : (t + 1) * TILE, :].reshape(FLAT, HD)
                for t, _ in users
            ],
            axis=1,
        )
        got = jnp.dot(hot, wide, preferred_element_type=f32)
        for n, (_, j) in enumerate(users):
            part = got[:, n * HD : (n + 1) * HD]
            if j in total:
                packed_ref[:, j * HD : (j + 1) * HD] = (total.pop(j) + part).astype(bf16)
            elif SLOTS * j // TILE != (SLOTS * j + SLOTS - 1) // TILE:
                total[j] = part
            else:
                packed_ref[:, j * HD : (j + 1) * HD] = part.astype(bf16)
    same = row_ref[...] == col_ref[...]
    core = core_ref[0]
    for side, out_ref in enumerate((own_ref, other_ref)):
        first = 3 * (core if side == 0 else 1 - core)
        for i in range(3):

            def block_at(base):
                at = pl.multiple_of((first + i + base) * HD, HD)
                return packed_ref[:, pl.ds(at, HD)]

            prob = soft(block_at(0), block_at(HEADS_HERE), same).astype(bf16)
            value = block_at(2 * HEADS_HERE)
            out_ref[:, i * HD : (i + 1) * HD] = jnp.dot(
                prob, value, preferred_element_type=f32
            ).astype(bf16)


def grad_near_kernel(own_cot, other_cot, own, up, down, swap, swap_up, swap_down, out_ref):
    terms = (
        (own_cot, 0, own),
        (own_cot, 1, up),
        (own_cot, 3, down),
        (other_cot, 0, swap),
        (other_cot, 1, swap_up),
        (other_cot, 3, swap_down),
    )
    total = None
    for cot, k, field in terms:
        product = jnp.dot(cot[k], field[...], preferred_element_type=f32)
        total = product if total is None else total + product
    out_ref[...] = total


def grad_far_kernel(own_cot, other_cot, own_far, swap_far, near_ref, out_ref):
    total = near_ref[...] + jnp.dot(own_cot[2], own_far[...], preferred_element_type=f32)
    total = total + jnp.dot(other_cot[2], swap_far[...], preferred_element_type=f32)
    out_ref[...] = total.astype(bf16).reshape(out_ref.shape)


def gram_kernel(parts_ref, grad_ref, gram_ref):
    grad = jnp.sum(parts_ref[...].astype(f32), axis=0)
    grad_ref[...] = grad
    for h in range(3):
        head = grad[:, h * HD : (h + 1) * HD]
        gram_ref[h * HD : (h + 1) * HD, :] = lax.dot_general(
            head,
            head,
            (((0,), (0,)), ((), ())),
            precision=lax.Precision.HIGHEST,
            preferred_element_type=f32,
        )


def update_kernel(core_ref, gram_ref, grad_ref, here_ref, there_ref, hold_ref):
    def mul(a, b):
        return jnp.dot(a, b, precision=lax.Precision.HIGHEST, preferred_element_type=f32)

    row = lax.broadcasted_iota(jnp.int32, (HD, HD), 0)
    col = lax.broadcasted_iota(jnp.int32, (HD, HD), 1)
    eye = jnp.where(row == col, 1.0, 0.0).astype(f32)
    grams, norms = [], []
    for h in range(3):
        gram = gram_ref[h * HD : (h + 1) * HD, :]
        norm = jnp.sqrt(jnp.sum(gram * eye, axis=(0, 1), keepdims=True)) + norm_eps
        grams.append(gram / norm / norm)
        norms.append(norm)
    results = [None] * 3
    for step in range(NS_STEPS):
        squares = [mul(g, g) for g in grams]
        mixers = [
            coef_a * eye + coef_b * g + coef_c * s for g, s in zip(grams, squares)
        ]
        results = [m if r is None else mul(r, m) for r, m in zip(results, mixers)]
        if step + 1 < NS_STEPS:
            grams = [mul(g, m) for g, m in zip(grams, mixers)]
            grams = [mul(g, m) for g, m in zip(grams, mixers)]
    for h in range(3):
        field = grad_ref[:, h * HD : (h + 1) * HD] / norms[h]
        final = mul(field, results[h]) * math.sqrt(D)
        hold_ref[:, :, h * HD : (h + 1) * HD] = final.reshape(C, FEAT, HD)
    core = core_ref[0]
    here_ref[...] = hold_ref[core]
    there_ref[...] = hold_ref[1 - core]


def join_kernel(core_ref, here_ref, there_ref, out_ref):
    core = core_ref[0]
    out_ref[:, pl.ds(pl.multiple_of(core * HALF, HD), HALF)] = here_ref[...]
    out_ref[:, pl.ds(pl.multiple_of((1 - core) * HALF, HD), HALF)] = there_ref[...]


def backward_kernel(row_ref, col_ref, q_ref, k_ref, v_ref, d0, d1, d2, d3, gq_ref, gk_ref, gv_ref):
    same = row_ref[...] == col_ref[...]
    q, k, v = q_ref[...], k_ref[...], v_ref[...]
    near = d0[...].astype(f32) + d1[...].astype(f32)
    d_out = (near + (d2[...].astype(f32) + d3[...].astype(f32))).astype(bf16)
    prob = soft(q, k, same)
    first = (((0,), (0,)), ((), ()))
    gv_ref[...] = lax.dot_general(
        prob.astype(bf16), d_out, first, preferred_element_type=f32
    ).astype(bf16)
    d_prob = lax.dot_general(d_out, v, (((1,), (1,)), ((), ())), preferred_element_type=f32)
    delta = jnp.sum(d_prob * prob, axis=-1, keepdims=True)
    d_score = (prob * (d_prob - delta) * scale).astype(bf16)
    gq_ref[...] = jnp.dot(d_score, k, preferred_element_type=f32).astype(bf16)
    gk_ref[...] = lax.dot_general(d_score, q, first, preferred_element_type=f32).astype(bf16)


def shift(field, axis, step):
    size = lax.axis_size(axis)
    return lax.ppermute(field, axis, [(i, (i + step) % size) for i in range(size)])


def local(kernel, name, out_shape, *operands, scalars=0, **options):
    smem = pl.BlockSpec(memory_space=pltpu.SMEM)
    vmem = pl.BlockSpec(memory_space=pltpu.VMEM)
    return pl.pallas_call(
        kernel,
        in_specs=[smem] * scalars + [vmem] * (len(operands) - scalars),
        out_shape=out_shape,
        compiler_params=pltpu.CompilerParams(vmem_limit_bytes=48 * 1024 * 1024),
        name=name,
        **options,
    )(*operands)


def array(shape, kind):
    return jax.ShapeDtypeStruct(shape, kind)


def shards(query, key, value, send_to, recv_from, segment, out_weight, cotangent):
    core = lax.axis_index("c")
    core_row = core.astype(jnp.int32).reshape(1)
    big = pltpu.CompilerParams(vmem_limit_bytes=48 * 1024 * 1024)
    everything = ("z", "y", "c")

    vmem = pl.BlockSpec(memory_space=pltpu.VMEM)
    hbm = pl.BlockSpec(memory_space=pltpu.HBM)
    field = pltpu.VMEM((ROWS, HEADS_HERE * HD), bf16)
    slots = pl.pallas_call(
        place_kernel,
        in_specs=[vmem, hbm, hbm, hbm],
        out_shape=array((GROUPS, TILES * TILE, HD), bf16),
        scratch_shapes=[field, field, field, pltpu.SemaphoreType.DMA((3,))],
        compiler_params=pltpu.CompilerParams(vmem_limit_bytes=60 * 1024 * 1024),
        name="place",
    )(send_to[None, :], query, key, value)
    arrived = lax.all_to_all(slots, everything, split_axis=0, concat_axis=0, tiled=True)

    cotangent, slots = lax.optimization_barrier((cotangent, slots))
    feature = jnp.arange(X * FEAT * Y, dtype=jnp.int32).reshape(2, Y, C, FEAT)
    feature = feature.transpose(1, 0, 2, 3).reshape(Y, -1)
    feature = jnp.roll(feature, -lax.axis_index("y"), axis=0).reshape(-1)
    perm = (feature[:, None] == jnp.arange(feature.size)[None, :]).astype(bf16)
    turned = lax.dot_general(
        perm, cotangent, (((1,), (1,)), ((), ())), preferred_element_type=f32
    ).astype(bf16)
    turned = turned.reshape(Y, 4 * FEAT, ROWS)
    turned = jnp.stack([turned[0]] + [shift(turned[k], "y", k) for k in range(1, Y)])
    cot_own = lax.all_gather(turned, "x", axis=1, tiled=True)
    cot_other = shift(cot_own, "c", 1)

    weight = lax.all_gather(out_weight, ("z", "c"), axis=0, tiled=True)
    part = array((ROWS, HEADS_HERE * HD), bf16)
    d_parts = local(parts_kernel, "d_parts", (part,) * Y, cot_own, weight)

    seg_row = segment[None, :]
    seg_col = segment[:, None]
    packed, own, other = local(
        forward_kernel,
        "forward",
        (
            array((ROWS, BLOCKS * HD), bf16),
            array((ROWS, HALF), bf16),
            array((ROWS, HALF), bf16),
        ),
        core_row,
        recv_from[None, :],
        recv_from[:, None],
        seg_row,
        seg_col,
        arrived,
        scalars=1,
    )

    own_up = shift(own, "y", 1)
    own_down = shift(own, "y", -1)
    swap = shift(other, "c", 1)
    swap_up = shift(swap, "y", 1)
    swap_down = shift(swap, "y", -1)
    own_far = shift(own_up, "y", 1)
    swap_far = shift(swap_down, "y", -1)
    grad = local(
        grad_near_kernel,
        "grad_near",
        array((Z * C * FEAT, HALF), f32),
        cot_own,
        cot_other,
        own,
        own_up,
        own_down,
        swap,
        swap_up,
        swap_down,
    )
    grad = local(
        grad_far_kernel,
        "grad_far",
        array((Z, C * FEAT, HALF), bf16),
        cot_own,
        cot_other,
        own_far,
        swap_far,
        grad,
    )
    parts = lax.all_to_all(grad, "z", split_axis=0, concat_axis=0, tiled=True)
    parts, *d_parts = lax.optimization_barrier((parts, *d_parts))
    d_parts = [d_parts[0]] + [shift(d_parts[k], "y", -k) for k in range(1, Y)]

    def column(base):
        return pl.BlockSpec((ROWS, HD), lambda h, base=base: (0, base + h))

    out = jax.ShapeDtypeStruct((ROWS, HEADS_HERE * HD), bf16)
    grads = pl.pallas_call(
        backward_kernel,
        grid=(HEADS_HERE,),
        in_specs=[
            pl.BlockSpec((1, ROWS), lambda h: (0, 0)),
            pl.BlockSpec((ROWS, 1), lambda h: (0, 0)),
            column(0),
            column(HEADS_HERE),
            column(2 * HEADS_HERE),
            column(0),
            column(0),
            column(0),
            column(0),
        ],
        out_specs=(column(0), column(0), column(0)),
        out_shape=(out, out, out),
        compiler_params=big,
        name="backward",
    )(seg_row, seg_col, packed, packed, packed, *d_parts)
    grad, gram = local(
        gram_kernel,
        "gram",
        (array((C * FEAT, HALF), f32), array((3 * HD, HD), f32)),
        parts,
    )
    gram = gram.reshape(Z, -1, HD)
    gram = jnp.sum(lax.all_to_all(gram, "z", split_axis=0, concat_axis=0, tiled=True), axis=0)
    gram = gram + lax.ppermute(gram, "y", [(i, i ^ 1) for i in range(Y)])
    gram = gram + lax.ppermute(gram, "y", [(i, Y - 1 - i) for i in range(Y)])
    gram = jnp.broadcast_to(gram[None], (Z, *gram.shape))
    gram = lax.all_to_all(gram, "z", split_axis=0, concat_axis=0, tiled=True)
    gram, *grads = lax.optimization_barrier((gram, *grads))
    half = array((FEAT, HALF), f32)
    here, there = local(
        update_kernel,
        "update",
        (half, half),
        core_row,
        gram.reshape(3 * HD, HD),
        grad,
        scalars=1,
        scratch_shapes=[pltpu.VMEM((C, FEAT, HALF), f32)],
    )
    there = shift(there, "c", 1)
    update = local(
        join_kernel, "join", array((FEAT, 2 * HALF), f32), core_row, here, there, scalars=1
    )

    return (*grads, update)


def solution(mesh):
    fine = Mesh(mesh.devices.reshape(Z, Y, C, X), ("z", "y", "c", "x"))
    everything = ("z", "y", "c")
    both = P(everything, "x")
    rows = P(everything)
    return jax.shard_map(
        shards,
        mesh=fine,
        in_specs=(both, both, both, rows, rows, rows, both, both),
        out_specs=(both, both, both, both),
        check_vma=False,
    )
```

```python
import math

import jax
import jax.numpy as jnp
from jax import lax
from jax.experimental import pallas as pl
from jax.experimental.pallas import tpu as pltpu
from jax.sharding import Mesh, PartitionSpec as P

D = 3072
HD = 128
ROWS = 256
GROUPS = 64
SLOTS = 6
HEADS_HERE = 6
BLOCKS = 3 * HEADS_HERE
TILE = 16
TILES = 7
FLAT = GROUPS * TILE
Z, Y, C, X = 8, 4, 2, 4
FEAT = 48
HALF = HEADS_HERE * HD // 2
NS_STEPS = 3

coef_a = 3.4445
coef_b = -4.775
coef_c = 2.0315
norm_eps = 1e-07
scale = 1.0 / math.sqrt(HD)
f32 = jnp.float32
bf16 = jnp.bfloat16


def find_patterns():
    found = []
    for tile in range(3):
        rows = [tile * TILE + i for i in range(TILE)]
        for block in sorted({r // SLOTS for r in rows}):
            found.append((tile, block))
    return found


PATTERNS = find_patterns()


def pattern_users(tile, block):
    return [
        (tile + 3 * n, block + 8 * n)
        for n in range(3)
        if tile + 3 * n < TILES and block + 8 * n < BLOCKS
    ]


def place_kernel(q_hbm, k_hbm, v_hbm, label_ref, out_ref, q_ref, k_ref, v_ref, sems):
    fields = (q_ref, k_ref, v_ref)
    copies = [
        pltpu.make_async_copy(source, target, sems.at[n])
        for n, (source, target) in enumerate(zip((q_hbm, k_hbm, v_hbm), fields))
    ]
    for copy in copies:
        copy.start()

    label = label_ref[...]
    group = lax.broadcasted_iota(jnp.int32, (GROUPS, ROWS), 0)
    before = jnp.sum(jnp.where(label < group, 1, 0), axis=1, keepdims=True)
    start = jnp.sum(jnp.where(label == group, before, 0), axis=0, keepdims=True)
    code = 8 * label + lax.broadcasted_iota(jnp.int32, (1, ROWS), 1) - start

    def block_of(j):
        return fields[j // HEADS_HERE][:, (j % HEADS_HERE) * HD : (j % HEADS_HERE + 1) * HD]

    row = lax.broadcasted_iota(jnp.int32, (TILE, ROWS), 0)
    eights = 8 * lax.broadcasted_iota(jnp.int32, (GROUPS, TILE, ROWS), 0)
    for copy in copies:
        copy.wait()
    for first in range(3):
        total = {}
        for tile, block in PATTERNS:
            if tile != first:
                continue
            slot = row + (TILE * tile - SLOTS * block)
            wanted = jnp.where((slot >= 0) & (slot < SLOTS), code - slot, -1)
            hot = jnp.where(eights == wanted[None], 1.0, 0.0).astype(bf16).reshape(FLAT, ROWS)
            users = pattern_users(tile, block)
            wide = jnp.concatenate([block_of(j) for _, j in users], axis=1)
            got = jnp.dot(hot, wide, preferred_element_type=f32)
            for n, (t, _) in enumerate(users):
                part = got[:, n * HD : (n + 1) * HD]
                total[t] = part if t not in total else total[t] + part
        for t, rows in total.items():
            out_ref[:, t * TILE : (t + 1) * TILE, :] = rows.astype(bf16).reshape(GROUPS, TILE, HD)


def join_cot_kernel(x_ref, *refs):
    *pieces, out_ref = refs
    for n, piece in enumerate(pieces):
        at = lax.rem(x_ref[0] + X - n % X, X) * (4 * FEAT)
        pair = n // X * 2
        out_ref[pair : pair + 2, pl.ds(pl.multiple_of(at, 4 * FEAT), 4 * FEAT), :] = piece[...]


def parts_kernel(cot_ref, weight_ref, *out_refs):
    weight = weight_ref[...]
    for k, out_ref in enumerate(out_refs):
        out_ref[...] = lax.dot_general(
            cot_ref[k], weight, (((0,), (0,)), ((), ())), preferred_element_type=f32
        ).astype(bf16)


def soft(q, k, same):
    scores = (
        lax.dot_general(q, k, (((1,), (1,)), ((), ())), preferred_element_type=f32) * scale
    )
    scores = jnp.where(same, scores, -jnp.inf)
    top = jnp.max(scores, axis=-1, keepdims=True)
    expo = jnp.exp(scores - top)
    return expo / jnp.sum(expo, axis=-1, keepdims=True)


def forward_kernel(
    core_ref,
    slots_hbm,
    from_row,
    from_col,
    row_ref,
    col_ref,
    packed_ref,
    own_ref,
    other_ref,
    slots_ref,
    sems,
):
    copies = []
    for t in range(TILES):
        rows = pl.ds(t * TILE, TILE)
        copies.append(pltpu.make_async_copy(slots_hbm.at[:, rows, :], slots_ref.at[t], sems.at[t]))
    for first in range(3):
        for copy in copies[first::3]:
            copy.start()

    before = jnp.sum(jnp.where(from_row[...] < from_col[...], 1, 0), axis=1, keepdims=True)
    code = 8 * from_col[...] + lax.broadcasted_iota(jnp.int32, (ROWS, 1), 0) - before
    lane = lax.broadcasted_iota(jnp.int32, (1, FLAT), 1)
    group = lane // TILE
    total = {}
    landed = set()
    for tile, block in PATTERNS:
        if tile not in landed:
            for copy in copies[tile::3]:
                copy.wait()
            landed.add(tile)
        slot = lane - TILE * group + (TILE * tile - SLOTS * block)
        wanted = jnp.where((slot >= 0) & (slot < SLOTS), 8 * group + slot, -1)
        hot = jnp.where(code == wanted, 1.0, 0.0).astype(bf16)
        users = pattern_users(tile, block)
        wide = jnp.concatenate(
            [slots_ref[t].reshape(FLAT, HD) for t, _ in users],
            axis=1,
        )
        got = jnp.dot(hot, wide, preferred_element_type=f32)
        for n, (_, j) in enumerate(users):
            part = got[:, n * HD : (n + 1) * HD]
            if j in total:
                packed_ref[:, j * HD : (j + 1) * HD] = (total.pop(j) + part).astype(bf16)
            elif SLOTS * j // TILE != (SLOTS * j + SLOTS - 1) // TILE:
                total[j] = part
            else:
                packed_ref[:, j * HD : (j + 1) * HD] = part.astype(bf16)
    same = row_ref[...] == col_ref[...]
    core = core_ref[0]
    for side, out_ref in enumerate((own_ref, other_ref)):
        first = 3 * (core if side == 0 else 1 - core)
        for i in range(3):

            def block_at(base):
                at = pl.multiple_of((first + i + base) * HD, HD)
                return packed_ref[:, pl.ds(at, HD)]

            prob = soft(block_at(0), block_at(HEADS_HERE), same).astype(bf16)
            value = block_at(2 * HEADS_HERE)
            out_ref[:, i * HD : (i + 1) * HD] = jnp.dot(
                prob, value, preferred_element_type=f32
            ).astype(bf16)


def grad_near_kernel(*refs):
    total = None
    for left, right in zip(refs[:6], refs[6:12]):
        product = jnp.dot(left[...], right[...], preferred_element_type=f32)
        total = product if total is None else total + product
    refs[12][...] = total


def grad_far_kernel(own_cot, other_cot, own_far, swap_far, near_ref, out_ref):
    total = near_ref[...] + jnp.dot(own_cot[...], own_far[...], preferred_element_type=f32)
    total = total + jnp.dot(other_cot[...], swap_far[...], preferred_element_type=f32)
    out_ref[...] = total.astype(bf16).reshape(out_ref.shape)


def gram_kernel(parts_ref, grad_ref, gram_ref):
    grad = jnp.sum(parts_ref[...].astype(f32), axis=0)
    grad_ref[...] = grad
    for h in range(3):
        head = grad[:, h * HD : (h + 1) * HD]
        gram_ref[h * HD : (h + 1) * HD, :] = lax.dot_general(
            head,
            head,
            (((0,), (0,)), ((), ())),
            precision=lax.Precision.HIGHEST,
            preferred_element_type=f32,
        )


def update_kernel(core_ref, gram_ref, grad_ref, here_ref, there_ref, hold_ref):
    def mul(a, b):
        return jnp.dot(a, b, precision=lax.Precision.HIGHEST, preferred_element_type=f32)

    row = lax.broadcasted_iota(jnp.int32, (HD, HD), 0)
    col = lax.broadcasted_iota(jnp.int32, (HD, HD), 1)
    eye = jnp.where(row == col, 1.0, 0.0).astype(f32)
    grams, norms = [], []
    for h in range(3):
        gram = gram_ref[h * HD : (h + 1) * HD, :]
        norm = jnp.sqrt(jnp.sum(gram * eye, axis=(0, 1), keepdims=True)) + norm_eps
        grams.append(gram / norm / norm)
        norms.append(norm)
    results = [None] * 3
    for step in range(NS_STEPS):
        squares = [mul(g, g) for g in grams]
        mixers = [
            coef_a * eye + coef_b * g + coef_c * s for g, s in zip(grams, squares)
        ]
        results = [m if r is None else mul(r, m) for r, m in zip(results, mixers)]
        if step + 1 < NS_STEPS:
            grams = [mul(g, m) for g, m in zip(grams, mixers)]
            grams = [mul(g, m) for g, m in zip(grams, mixers)]
    for h in range(3):
        field = grad_ref[:, h * HD : (h + 1) * HD] / norms[h]
        final = mul(field, results[h]) * math.sqrt(D)
        hold_ref[:, :, h * HD : (h + 1) * HD] = final.reshape(C, FEAT, HD)
    core = core_ref[0]
    here_ref[...] = hold_ref[core]
    there_ref[...] = hold_ref[1 - core]


def join_kernel(core_ref, here_ref, there_ref, out_ref):
    core = core_ref[0]
    out_ref[:, pl.ds(pl.multiple_of(core * HALF, HD), HALF)] = here_ref[...]
    out_ref[:, pl.ds(pl.multiple_of((1 - core) * HALF, HD), HALF)] = there_ref[...]


def backward_kernel(row_ref, col_ref, q_ref, k_ref, v_ref, d0, d1, d2, d3, *refs):
    gq_ref, gk_ref, gv_ref = refs[-3:]
    same = row_ref[...] == col_ref[...]
    q, k, v = q_ref[...], k_ref[...], v_ref[...]
    near = d0[...].astype(f32) + d1[...].astype(f32)
    d_out = (near + (d2[...].astype(f32) + d3[...].astype(f32))).astype(bf16)
    prob = soft(q, k, same)
    first = (((0,), (0,)), ((), ()))
    gv_ref[...] = lax.dot_general(
        prob.astype(bf16), d_out, first, preferred_element_type=f32
    ).astype(bf16)
    d_prob = lax.dot_general(d_out, v, (((1,), (1,)), ((), ())), preferred_element_type=f32)
    delta = jnp.sum(d_prob * prob, axis=-1, keepdims=True)
    d_score = (prob * (d_prob - delta) * scale).astype(bf16)
    gq_ref[...] = jnp.dot(d_score, k, preferred_element_type=f32).astype(bf16)
    gk_ref[...] = lax.dot_general(d_score, q, first, preferred_element_type=f32).astype(bf16)


def shift(field, axis, step):
    size = lax.axis_size(axis)
    return lax.ppermute(field, axis, [(i, (i + step) % size) for i in range(size)])


def cross(field, step):
    pairs = [(y * C + c, (y + step) % Y * C + 1 - c) for y in range(Y) for c in range(C)]
    return lax.ppermute(field, ("y", "c"), pairs)


def local(kernel, name, out_shape, *operands, scalars=0, far=0, room=24, **options):
    smem = pl.BlockSpec(memory_space=pltpu.SMEM)
    vmem = pl.BlockSpec(memory_space=pltpu.VMEM)
    hbm = pl.BlockSpec(memory_space=pltpu.HBM)
    return pl.pallas_call(
        kernel,
        in_specs=[smem] * scalars + [hbm] * far + [vmem] * (len(operands) - scalars - far),
        out_shape=out_shape,
        compiler_params=pltpu.CompilerParams(vmem_limit_bytes=room * 1024 * 1024),
        name=name,
        **options,
    )(*operands)


def array(shape, kind):
    return jax.ShapeDtypeStruct(shape, kind)


def shards(query, key, value, send_to, recv_from, segment, out_weight, cotangent):
    core = lax.axis_index("c")
    core_row = core.astype(jnp.int32).reshape(1)
    everything = ("z", "y", "c")

    field = pltpu.VMEM((ROWS, HEADS_HERE * HD), bf16)
    slots = local(
        place_kernel,
        "place",
        array((GROUPS, TILES * TILE, HD), bf16),
        query,
        key,
        value,
        send_to[None, :],
        far=3,
        room=60,
        scratch_shapes=[field, field, field, pltpu.SemaphoreType.DMA((3,))],
    )
    arrived = lax.all_to_all(slots, everything, split_axis=0, concat_axis=0, tiled=True)

    cotangent, slots = lax.optimization_barrier((cotangent, slots))
    feature = jnp.arange(X * FEAT * Y, dtype=jnp.int32).reshape(2, Y, C, FEAT)
    feature = feature.transpose(1, 0, 2, 3).reshape(Y, -1)
    feature = jnp.roll(feature, -lax.axis_index("y"), axis=0).reshape(-1)
    perm = (feature[:, None] == jnp.arange(feature.size)[None, :]).astype(bf16)
    turned = lax.dot_general(
        perm, cotangent, (((1,), (1,)), ((), ())), preferred_element_type=f32
    ).astype(bf16)
    turned = turned.reshape(Y, 4 * FEAT, ROWS)
    turned = [turned[0]] + [shift(turned[k], "y", k) for k in range(1, Y)]
    one, two = jnp.stack(turned[:2]), jnp.stack(turned[2:])
    one_up, two_down = shift(one, "x", 1), shift(two, "x", -1)
    two_up, one_down = shift(two, "x", 1), shift(one, "x", -1)
    one_far, two_far = shift(one_up, "x", 1), shift(two_down, "x", -1)
    cot_own = local(
        join_cot_kernel,
        "join_cot",
        array((Y, X * 4 * FEAT, ROWS), bf16),
        lax.axis_index("x").astype(jnp.int32).reshape(1),
        one,
        one_up,
        one_far,
        one_down,
        two,
        two_up,
        two_far,
        two_down,
        scalars=1,
        room=60,
    )
    cot_other = shift(cot_own, "c", 1)

    weight = lax.all_gather(out_weight, ("z", "c"), axis=0, tiled=True)
    part = array((ROWS, HEADS_HERE * HD), bf16)
    work = pl.CostEstimate(flops=18 * 10**9, bytes_accessed=54 * 10**6, transcendentals=0)
    d_parts = local(parts_kernel, "d_parts", (part,) * Y, cot_own, weight, room=60, cost_estimate=work)
    arrived, cot_own, cot_other, *d_parts = lax.optimization_barrier(
        (arrived, cot_own, cot_other, *d_parts)
    )

    seg_row = segment[None, :]
    seg_col = segment[:, None]
    packed, own, other = local(
        forward_kernel,
        "forward",
        (
            array((ROWS, BLOCKS * HD), bf16),
            array((ROWS, HALF), bf16),
            array((ROWS, HALF), bf16),
        ),
        core_row,
        arrived,
        recv_from[None, :],
        recv_from[:, None],
        seg_row,
        seg_col,
        scalars=1,
        far=1,
        scratch_shapes=[
            pltpu.VMEM((TILES, GROUPS, TILE, HD), bf16),
            pltpu.SemaphoreType.DMA((TILES,)),
        ],
    )

    own_up = shift(own, "y", 1)
    own_down = shift(own, "y", -1)
    swap = shift(other, "c", 1)
    swap_up = cross(other, 1)
    swap_down = cross(other, -1)
    own_far = shift(own_up, "y", 1)
    swap_far = shift(swap_down, "y", -1)
    grad = local(
        grad_near_kernel,
        "grad_near",
        array((Z * C * FEAT, HALF), f32),
        *[cot_own[k] for k in (0, 1, 3)],
        *[cot_other[k] for k in (0, 1, 3)],
        own,
        own_up,
        own_down,
        swap,
        swap_up,
        swap_down,
    )
    grad = local(
        grad_far_kernel,
        "grad_far",
        array((Z, C * FEAT, HALF), bf16),
        cot_own[2],
        cot_other[2],
        own_far,
        swap_far,
        grad,
    )
    grad, *d_parts = lax.optimization_barrier((grad, *d_parts))
    d_parts = [d_parts[0]] + [shift(d_parts[k], "y", -k) for k in range(1, Y)]
    parts = lax.all_to_all(grad, "z", split_axis=0, concat_axis=0, tiled=True)

    out = array((ROWS, HEADS_HERE * HD), bf16)

    def backward(heads, held):
        def column(base):
            return pl.BlockSpec((ROWS, HD), lambda h: (0, base + heads + h))

        return pl.pallas_call(
            backward_kernel,
            grid=(3,),
            in_specs=[
                pl.BlockSpec((1, ROWS), lambda h: (0, 0)),
                pl.BlockSpec((ROWS, 1), lambda h: (0, 0)),
                column(0),
                column(HEADS_HERE),
                column(2 * HEADS_HERE),
                *[column(0)] * Y,
                *[pl.BlockSpec(memory_space=pl.ANY)] * len(held),
            ],
            out_specs=(column(0),) * 3,
            out_shape=(out,) * 3,
            input_output_aliases={5 + Y + n: n for n in range(len(held))},
            compiler_params=pltpu.CompilerParams(vmem_limit_bytes=24 * 1024 * 1024),
            name="backward",
        )(seg_row, seg_col, packed, packed, packed, *d_parts, *held)

    grads = backward(0, ())

    grad, gram = local(
        gram_kernel,
        "gram",
        (array((C * FEAT, HALF), f32), array((3 * HD, HD), f32)),
        parts,
    )
    gram = gram.reshape(Z, -1, HD)
    gram = jnp.sum(lax.all_to_all(gram, "z", split_axis=0, concat_axis=0, tiled=True), axis=0)
    gram, *grads = lax.optimization_barrier((gram, *grads))
    gram = sum([shift(gram, "y", k) for k in range(1, Y)], gram)
    gram = jnp.broadcast_to(gram[None], (Z, *gram.shape))
    gram = lax.all_to_all(gram, "z", split_axis=0, concat_axis=0, tiled=True)
    grads = backward(3, grads)
    gram, *grads = lax.optimization_barrier((gram, *grads))
    half = array((FEAT, HALF), f32)
    here, there = local(
        update_kernel,
        "update",
        (half, half),
        core_row,
        gram.reshape(3 * HD, HD),
        grad,
        scalars=1,
        scratch_shapes=[pltpu.VMEM((C, FEAT, HALF), f32)],
    )
    there = shift(there, "c", 1)
    update = local(
        join_kernel, "join", array((FEAT, 2 * HALF), f32), core_row, here, there, scalars=1
    )

    return (*grads, update)


def solution(mesh):
    fine = Mesh(mesh.devices.reshape(Z, Y, C, X), ("z", "y", "c", "x"))
    everything = ("z", "y", "c")
    both = P(everything, "x")
    rows = P(everything)
    return jax.shard_map(
        shards,
        mesh=fine,
        in_specs=(both, both, both, rows, rows, rows, both, both),
        out_specs=(both, both, both, both),
        check_vma=False,
    )
```

```python
import math

import jax
import jax.numpy as jnp
from jax import lax
from jax.experimental import pallas as pl
from jax.experimental.pallas import tpu as pltpu
from jax.sharding import Mesh, PartitionSpec as P

D = 3072
HD = 128
ROWS = 256
GROUPS = 64
SLOTS = 6
HEADS_HERE = 6
BLOCKS = 3 * HEADS_HERE
TILE = 16
TILES = 7
EIGHT = 8
FLAT = GROUPS * EIGHT
Z, Y, C, X = 8, 4, 2, 4
FEAT = 48
HALF = HEADS_HERE * HD // 2
NS_STEPS = 3

coef_a = 3.4445
coef_b = -4.775
coef_c = 2.0315
norm_eps = 1e-07
scale = 1.0 / math.sqrt(HD)
f32 = jnp.float32
bf16 = jnp.bfloat16


def place_kernel(q_hbm, k_hbm, v_hbm, label_ref, out_ref, q_ref, k_ref, v_ref, sems):
    fields = (q_ref, k_ref, v_ref)
    copies = [
        pltpu.make_async_copy(source, target, sems.at[n])
        for n, (source, target) in enumerate(zip((q_hbm, k_hbm, v_hbm), fields))
    ]
    for copy in copies:
        copy.start()

    label = label_ref[...]
    group = lax.broadcasted_iota(jnp.int32, (GROUPS, ROWS), 0)
    before = jnp.sum(jnp.where(label < group, 1, 0), axis=1, keepdims=True)
    start = jnp.sum(jnp.where(label == group, before, 0), axis=0, keepdims=True)
    code = 8 * label + lax.broadcasted_iota(jnp.int32, (1, ROWS), 1) - start

    row = lax.broadcasted_iota(jnp.int32, (FLAT, ROWS), 0)
    hot = jnp.where(row == code, 1.0, 0.0).astype(bf16)
    place = lax.broadcasted_iota(jnp.int32, (GROUPS, EIGHT, HD), 1)
    rolled = [None] * BLOCKS
    tiles = []
    for pair in range(BLOCKS // 2):
        which, at = divmod(pair, 3)
        if at == 0:
            copies[which].wait()
        wide = fields[which][:, at * 2 * HD : (at + 1) * 2 * HD]
        got = jnp.dot(hot, wide, preferred_element_type=f32)
        for j in (2 * pair, 2 * pair + 1):
            block = got[:, j % 2 * HD : (j % 2 + 1) * HD].reshape(GROUPS, EIGHT, HD)
            rolled[j] = pltpu.roll(block, SLOTS * j % EIGHT, 1) if SLOTS * j % EIGHT else block
        while len(tiles) < 2 * TILES:
            j = EIGHT * len(tiles) // SLOTS
            later = j + 1 if j + 1 < BLOCKS else j
            if rolled[later] is None:
                break
            split = SLOTS * (j + 1) - EIGHT * len(tiles)
            rest = rolled[later] if later > j else 0.0
            tiles.append(jnp.where(place < split, rolled[j], rest))
            if len(tiles) % 2 == 0:
                t = len(tiles) // 2 - 1
                both = jnp.concatenate(tiles[-2:], axis=1)
                out_ref[:, t * TILE : (t + 1) * TILE, :] = both.astype(bf16)


def join_cot_kernel(x_ref, *refs):
    *pieces, out_ref = refs
    for n, piece in enumerate(pieces):
        at = lax.rem(x_ref[0] + X - n % X, X) * (4 * FEAT)
        pair = n // X * 2
        out_ref[pair : pair + 2, pl.ds(pl.multiple_of(at, 4 * FEAT), 4 * FEAT), :] = piece[...]


def parts_kernel(cot_ref, weight_ref, *out_refs):
    weight = weight_ref[...]
    for k, out_ref in enumerate(out_refs):
        out_ref[...] = lax.dot_general(
            cot_ref[k], weight, (((0,), (0,)), ((), ())), preferred_element_type=f32
        ).astype(bf16)


def soft(q, k, same):
    scores = (
        lax.dot_general(q, k, (((1,), (1,)), ((), ())), preferred_element_type=f32) * scale
    )
    scores = jnp.where(same, scores, -jnp.inf)
    top = jnp.max(scores, axis=-1, keepdims=True)
    expo = jnp.exp(scores - top)
    return expo / jnp.sum(expo, axis=-1, keepdims=True)


def forward_kernel(
    core_ref, slots_ref, from_row, from_col, row_ref, col_ref, packed_ref, own_ref, other_ref
):
    before = jnp.sum(jnp.where(from_row[...] < from_col[...], 1, 0), axis=1, keepdims=True)
    code = 8 * from_col[...] + lax.broadcasted_iota(jnp.int32, (ROWS, 1), 0) - before
    lane = lax.broadcasted_iota(jnp.int32, (ROWS, FLAT), 1)
    hot = jnp.where(code == lane, 1.0, 0.0).astype(bf16)
    place = lax.broadcasted_iota(jnp.int32, (GROUPS, EIGHT, HD), 1)
    tiles = []
    for t in range(TILES):
        both = slots_ref[:, t * TILE : (t + 1) * TILE, :].astype(f32)
        tiles += [both[:, :EIGHT], both[:, EIGHT:]]
    for pair in range(BLOCKS // 2):
        blocks = []
        for j in (2 * pair, 2 * pair + 1):
            t, start = divmod(SLOTS * j, EIGHT)
            block = tiles[t]
            if start + SLOTS > EIGHT:
                block = jnp.where(place < start, tiles[t + 1], block)
            if start:
                block = pltpu.roll(block, EIGHT - start, 1)
            blocks.append(block.reshape(FLAT, HD).astype(bf16))
        wide = jnp.concatenate(blocks, axis=1)
        got = jnp.dot(hot, wide, preferred_element_type=f32)
        packed_ref[:, pair * 2 * HD : (pair + 1) * 2 * HD] = got.astype(bf16)
    same = row_ref[...] == col_ref[...]
    core = core_ref[0]
    for side, out_ref in enumerate((own_ref, other_ref)):
        first = 3 * (core if side == 0 else 1 - core)
        for i in range(3):

            def block_at(base):
                at = pl.multiple_of((first + i + base) * HD, HD)
                return packed_ref[:, pl.ds(at, HD)]

            prob = soft(block_at(0), block_at(HEADS_HERE), same).astype(bf16)
            value = block_at(2 * HEADS_HERE)
            out_ref[:, i * HD : (i + 1) * HD] = jnp.dot(
                prob, value, preferred_element_type=f32
            ).astype(bf16)


def grad_near_kernel(*refs):
    total = None
    for left, right in zip(refs[:6], refs[6:12]):
        product = jnp.dot(left[...], right[...], preferred_element_type=f32)
        total = product if total is None else total + product
    refs[12][...] = total


def grad_far_kernel(own_cot, other_cot, own_far, swap_far, near_ref, out_ref):
    total = near_ref[...] + jnp.dot(own_cot[...], own_far[...], preferred_element_type=f32)
    total = total + jnp.dot(other_cot[...], swap_far[...], preferred_element_type=f32)
    out_ref[...] = total.astype(bf16).reshape(out_ref.shape)


def gram_kernel(parts_ref, grad_ref, gram_ref):
    grad = jnp.sum(parts_ref[...].astype(f32), axis=0)
    grad_ref[...] = grad
    for h in range(3):
        head = grad[:, h * HD : (h + 1) * HD]
        gram_ref[h * HD : (h + 1) * HD, :] = lax.dot_general(
            head,
            head,
            (((0,), (0,)), ((), ())),
            precision=lax.Precision.HIGHEST,
            preferred_element_type=f32,
        )


def update_kernel(core_ref, gram_ref, grad_ref, here_ref, there_ref, hold_ref):
    def mul(a, b):
        return jnp.dot(a, b, precision=lax.Precision.HIGHEST, preferred_element_type=f32)

    row = lax.broadcasted_iota(jnp.int32, (HD, HD), 0)
    col = lax.broadcasted_iota(jnp.int32, (HD, HD), 1)
    eye = jnp.where(row == col, 1.0, 0.0).astype(f32)
    grams, norms = [], []
    for h in range(3):
        gram = gram_ref[h * HD : (h + 1) * HD, :]
        norm = jnp.sqrt(jnp.sum(gram * eye, axis=(0, 1), keepdims=True)) + norm_eps
        grams.append(gram / norm / norm)
        norms.append(norm)
    results = [None] * 3
    for step in range(NS_STEPS):
        squares = [mul(g, g) for g in grams]
        mixers = [
            coef_a * eye + coef_b * g + coef_c * s for g, s in zip(grams, squares)
        ]
        results = [m if r is None else mul(r, m) for r, m in zip(results, mixers)]
        if step + 1 < NS_STEPS:
            grams = [mul(g, m) for g, m in zip(grams, mixers)]
            grams = [mul(g, m) for g, m in zip(grams, mixers)]
    for h in range(3):
        field = grad_ref[:, h * HD : (h + 1) * HD] / norms[h]
        final = mul(field, results[h]) * math.sqrt(D)
        hold_ref[:, :, h * HD : (h + 1) * HD] = final.reshape(C, FEAT, HD)
    core = core_ref[0]
    here_ref[...] = hold_ref[core]
    there_ref[...] = hold_ref[1 - core]


def join_kernel(core_ref, here_ref, there_ref, out_ref):
    core = core_ref[0]
    out_ref[:, pl.ds(pl.multiple_of(core * HALF, HD), HALF)] = here_ref[...]
    out_ref[:, pl.ds(pl.multiple_of((1 - core) * HALF, HD), HALF)] = there_ref[...]


def backward_kernel(row_ref, col_ref, q_ref, k_ref, v_ref, d0, d1, d2, d3, *refs):
    gq_ref, gk_ref, gv_ref = refs[-3:]
    same = row_ref[...] == col_ref[...]
    q, k, v = q_ref[...], k_ref[...], v_ref[...]
    near = d0[...].astype(f32) + d1[...].astype(f32)
    d_out = (near + (d2[...].astype(f32) + d3[...].astype(f32))).astype(bf16)
    prob = soft(q, k, same)
    first = (((0,), (0,)), ((), ()))
    gv_ref[...] = lax.dot_general(
        prob.astype(bf16), d_out, first, preferred_element_type=f32
    ).astype(bf16)
    d_prob = lax.dot_general(d_out, v, (((1,), (1,)), ((), ())), preferred_element_type=f32)
    delta = jnp.sum(d_prob * prob, axis=-1, keepdims=True)
    d_score = (prob * (d_prob - delta) * scale).astype(bf16)
    gq_ref[...] = jnp.dot(d_score, k, preferred_element_type=f32).astype(bf16)
    gk_ref[...] = lax.dot_general(d_score, q, first, preferred_element_type=f32).astype(bf16)


def shift(field, axis, step):
    size = lax.axis_size(axis)
    return lax.ppermute(field, axis, [(i, (i + step) % size) for i in range(size)])


def cross(field, step):
    pairs = [(y * C + c, (y + step) % Y * C + 1 - c) for y in range(Y) for c in range(C)]
    return lax.ppermute(field, ("y", "c"), pairs)


def local(kernel, name, out_shape, *operands, scalars=0, far=0, room=24, **options):
    smem = pl.BlockSpec(memory_space=pltpu.SMEM)
    vmem = pl.BlockSpec(memory_space=pltpu.VMEM)
    hbm = pl.BlockSpec(memory_space=pltpu.HBM)
    return pl.pallas_call(
        kernel,
        in_specs=[smem] * scalars + [hbm] * far + [vmem] * (len(operands) - scalars - far),
        out_shape=out_shape,
        compiler_params=pltpu.CompilerParams(vmem_limit_bytes=room * 1024 * 1024),
        name=name,
        **options,
    )(*operands)


def array(shape, kind):
    return jax.ShapeDtypeStruct(shape, kind)


def shards(query, key, value, send_to, recv_from, segment, out_weight, cotangent):
    core = lax.axis_index("c")
    core_row = core.astype(jnp.int32).reshape(1)
    everything = ("z", "y", "c")

    field = pltpu.VMEM((ROWS, HEADS_HERE * HD), bf16)
    slots = local(
        place_kernel,
        "place",
        array((GROUPS, TILES * TILE, HD), bf16),
        query,
        key,
        value,
        send_to[None, :],
        far=3,
        room=60,
        scratch_shapes=[field, field, field, pltpu.SemaphoreType.DMA((3,))],
    )
    arrived = lax.all_to_all(slots, everything, split_axis=0, concat_axis=0, tiled=True)

    cotangent, slots = lax.optimization_barrier((cotangent, slots))
    feature = jnp.arange(X * FEAT * Y, dtype=jnp.int32).reshape(2, Y, C, FEAT)
    feature = feature.transpose(1, 0, 2, 3).reshape(Y, -1)
    feature = jnp.roll(feature, -lax.axis_index("y"), axis=0).reshape(-1)
    perm = (feature[:, None] == jnp.arange(feature.size)[None, :]).astype(bf16)
    turned = lax.dot_general(
        perm, cotangent, (((1,), (1,)), ((), ())), preferred_element_type=f32
    ).astype(bf16)
    turned = turned.reshape(Y, 4 * FEAT, ROWS)
    turned = [turned[0]] + [shift(turned[k], "y", k) for k in range(1, Y)]
    one, two = jnp.stack(turned[:2]), jnp.stack(turned[2:])
    one_up, two_down = shift(one, "x", 1), shift(two, "x", -1)
    two_up, one_down = shift(two, "x", 1), shift(one, "x", -1)
    one_far, two_far = shift(one_up, "x", 1), shift(two_down, "x", -1)
    cot_own = local(
        join_cot_kernel,
        "join_cot",
        array((Y, X * 4 * FEAT, ROWS), bf16),
        lax.axis_index("x").astype(jnp.int32).reshape(1),
        one,
        one_up,
        one_far,
        one_down,
        two,
        two_up,
        two_far,
        two_down,
        scalars=1,
        room=60,
    )
    cot_other = shift(cot_own, "c", 1)

    weight = lax.all_gather(out_weight, ("z", "c"), axis=0, tiled=True)
    part = array((ROWS, HEADS_HERE * HD), bf16)
    work = pl.CostEstimate(flops=18 * 10**9, bytes_accessed=54 * 10**6, transcendentals=0)
    d_parts = local(parts_kernel, "d_parts", (part,) * Y, cot_own, weight, room=60, cost_estimate=work)
    arrived, cot_own, cot_other, *d_parts = lax.optimization_barrier(
        (arrived, cot_own, cot_other, *d_parts)
    )

    seg_row = segment[None, :]
    seg_col = segment[:, None]
    packed, own, other = local(
        forward_kernel,
        "forward",
        (
            array((ROWS, BLOCKS * HD), bf16),
            array((ROWS, HALF), bf16),
            array((ROWS, HALF), bf16),
        ),
        core_row,
        arrived,
        recv_from[None, :],
        recv_from[:, None],
        seg_row,
        seg_col,
        scalars=1,
    )

    own_up = shift(own, "y", 1)
    own_down = shift(own, "y", -1)
    swap = shift(other, "c", 1)
    swap_up = cross(other, 1)
    swap_down = cross(other, -1)
    own_far = shift(own_up, "y", 1)
    swap_far = shift(swap_down, "y", -1)
    grad = local(
        grad_near_kernel,
        "grad_near",
        array((Z * C * FEAT, HALF), f32),
        *[cot_own[k] for k in (0, 1, 3)],
        *[cot_other[k] for k in (0, 1, 3)],
        own,
        own_up,
        own_down,
        swap,
        swap_up,
        swap_down,
    )
    grad = local(
        grad_far_kernel,
        "grad_far",
        array((Z, C * FEAT, HALF), bf16),
        cot_own[2],
        cot_other[2],
        own_far,
        swap_far,
        grad,
    )
    grad, *d_parts = lax.optimization_barrier((grad, *d_parts))
    d_parts = [d_parts[0]] + [shift(d_parts[k], "y", -k) for k in range(1, Y)]
    parts = lax.all_to_all(grad, "z", split_axis=0, concat_axis=0, tiled=True)

    out = array((ROWS, HEADS_HERE * HD), bf16)

    def backward(heads, held):
        def column(base):
            return pl.BlockSpec((ROWS, HD), lambda h: (0, base + heads + h))

        return pl.pallas_call(
            backward_kernel,
            grid=(3,),
            in_specs=[
                pl.BlockSpec((1, ROWS), lambda h: (0, 0)),
                pl.BlockSpec((ROWS, 1), lambda h: (0, 0)),
                column(0),
                column(HEADS_HERE),
                column(2 * HEADS_HERE),
                *[column(0)] * Y,
                *[pl.BlockSpec(memory_space=pl.ANY)] * len(held),
            ],
            out_specs=(column(0),) * 3,
            out_shape=(out,) * 3,
            input_output_aliases={5 + Y + n: n for n in range(len(held))},
            compiler_params=pltpu.CompilerParams(vmem_limit_bytes=24 * 1024 * 1024),
            name="backward",
        )(seg_row, seg_col, packed, packed, packed, *d_parts, *held)

    grads = backward(0, ())

    grad, gram = local(
        gram_kernel,
        "gram",
        (array((C * FEAT, HALF), f32), array((3 * HD, HD), f32)),
        parts,
    )
    gram = gram.reshape(Z, -1, HD)
    gram = jnp.sum(lax.all_to_all(gram, "z", split_axis=0, concat_axis=0, tiled=True), axis=0)
    gram, *grads = lax.optimization_barrier((gram, *grads))
    gram = sum([shift(gram, "y", k) for k in range(1, Y)], gram)
    gram = jnp.broadcast_to(gram[None], (Z, *gram.shape))
    gram = lax.all_to_all(gram, "z", split_axis=0, concat_axis=0, tiled=True)
    grads = backward(3, grads)
    gram, *grads = lax.optimization_barrier((gram, *grads))
    half = array((FEAT, HALF), f32)
    here, there = local(
        update_kernel,
        "update",
        (half, half),
        core_row,
        gram.reshape(3 * HD, HD),
        grad,
        scalars=1,
        scratch_shapes=[pltpu.VMEM((C, FEAT, HALF), f32)],
    )
    there = shift(there, "c", 1)
    update = local(
        join_kernel, "join", array((FEAT, 2 * HALF), f32), core_row, here, there, scalars=1
    )

    return (*grads, update)


def solution(mesh):
    fine = Mesh(mesh.devices.reshape(Z, Y, C, X), ("z", "y", "c", "x"))
    everything = ("z", "y", "c")
    both = P(everything, "x")
    rows = P(everything)
    return jax.shard_map(
        shards,
        mesh=fine,
        in_specs=(both, both, both, rows, rows, rows, both, both),
        out_specs=(both, both, both, both),
        check_vma=False,
    )
```

```python
import math

import jax
import jax.numpy as jnp
from jax import lax
from jax.experimental import pallas as pl
from jax.experimental.pallas import tpu as pltpu
from jax.sharding import Mesh, PartitionSpec as P

D = 3072
HD = 128
ROWS = 256
GROUPS = 64
SLOTS = 6
HEADS_HERE = 6
BLOCKS = 3 * HEADS_HERE
TILE = 16
TILES = 7
EIGHT = 8
FLAT = GROUPS * EIGHT
Z, Y, C, X = 8, 4, 2, 4
FEAT = 48
HALF = HEADS_HERE * HD // 2
NS_STEPS = 3

coef_a = 3.4445
coef_b = -4.775
coef_c = 2.0315
norm_eps = 1e-07
scale = 1.0 / math.sqrt(HD)
f32 = jnp.float32
bf16 = jnp.bfloat16


def place_kernel(q_hbm, k_hbm, v_hbm, label_ref, out_ref, q_ref, k_ref, v_ref, sems):
    fields = (q_ref, k_ref, v_ref)
    copies = [
        pltpu.make_async_copy(source, target, sems.at[n])
        for n, (source, target) in enumerate(zip((q_hbm, k_hbm, v_hbm), fields))
    ]
    for copy in copies:
        copy.start()

    label = label_ref[...]
    group = lax.broadcasted_iota(jnp.int32, (GROUPS, ROWS), 0)
    before = jnp.sum(jnp.where(label < group, 1, 0), axis=1, keepdims=True)
    start = jnp.sum(jnp.where(label == group, before, 0), axis=0, keepdims=True)
    code = 8 * label + lax.broadcasted_iota(jnp.int32, (1, ROWS), 1) - start

    row = lax.broadcasted_iota(jnp.int32, (FLAT, ROWS), 0)
    hot = jnp.where(row == code, 1.0, 0.0).astype(bf16)
    place = lax.broadcasted_iota(jnp.int32, (GROUPS, EIGHT, HD), 1)
    rolled = [None] * BLOCKS
    tiles = []
    for pair in range(BLOCKS // 2):
        which, at = divmod(pair, 3)
        if at == 0:
            copies[which].wait()
        wide = fields[which][:, at * 2 * HD : (at + 1) * 2 * HD]
        got = jnp.dot(hot, wide, preferred_element_type=f32)
        for j in (2 * pair, 2 * pair + 1):
            block = got[:, j % 2 * HD : (j % 2 + 1) * HD].reshape(GROUPS, EIGHT, HD)
            rolled[j] = pltpu.roll(block, SLOTS * j % EIGHT, 1) if SLOTS * j % EIGHT else block
        while len(tiles) < 2 * TILES:
            j = EIGHT * len(tiles) // SLOTS
            later = j + 1 if j + 1 < BLOCKS else j
            if rolled[later] is None:
                break
            split = SLOTS * (j + 1) - EIGHT * len(tiles)
            rest = rolled[later] if later > j else 0.0
            tiles.append(jnp.where(place < split, rolled[j], rest))
            if len(tiles) % 2 == 0:
                t = len(tiles) // 2 - 1
                both = jnp.concatenate(tiles[-2:], axis=1)
                out_ref[:, t * TILE : (t + 1) * TILE, :] = both.astype(bf16)


def join_cot_kernel(x_ref, *refs):
    *pieces, out_ref = refs
    for n, piece in enumerate(pieces):
        at = lax.rem(x_ref[0] + X - n % X, X) * (4 * FEAT)
        pair = n // X * 2
        out_ref[pair : pair + 2, pl.ds(pl.multiple_of(at, 4 * FEAT), 4 * FEAT), :] = piece[...]


def parts_kernel(cot_ref, weight_ref, *out_refs):
    weight = weight_ref[...]
    for k, out_ref in zip((0, 1, 3), out_refs):
        out_ref[...] = lax.dot_general(
            cot_ref[k], weight, (((0,), (0,)), ((), ())), preferred_element_type=f32
        ).astype(bf16)
    far = lax.dot_general(
        cot_ref[2], weight, (((0,), (0,)), ((), ())), preferred_element_type=f32
    ).astype(bf16)
    out_refs[3][...] = far[: ROWS // 2]
    out_refs[4][...] = far[ROWS // 2 :]


def soft(q, k, same):
    scores = (
        lax.dot_general(q, k, (((1,), (1,)), ((), ())), preferred_element_type=f32) * scale
    )
    scores = jnp.where(same, scores, -jnp.inf)
    top = jnp.max(scores, axis=-1, keepdims=True)
    expo = jnp.exp(scores - top)
    return expo / jnp.sum(expo, axis=-1, keepdims=True)


def forward_kernel(
    core_ref, slots_ref, from_row, from_col, row_ref, col_ref, packed_ref, own_ref, other_ref
):
    before = jnp.sum(jnp.where(from_row[...] < from_col[...], 1, 0), axis=1, keepdims=True)
    code = 8 * from_col[...] + lax.broadcasted_iota(jnp.int32, (ROWS, 1), 0) - before
    lane = lax.broadcasted_iota(jnp.int32, (ROWS, FLAT), 1)
    hot = jnp.where(code == lane, 1.0, 0.0).astype(bf16)
    place = lax.broadcasted_iota(jnp.int32, (GROUPS, EIGHT, HD), 1)
    tiles = []
    for t in range(TILES):
        both = slots_ref[:, t * TILE : (t + 1) * TILE, :].astype(f32)
        tiles += [both[:, :EIGHT], both[:, EIGHT:]]
    for pair in range(BLOCKS // 2):
        blocks = []
        for j in (2 * pair, 2 * pair + 1):
            t, start = divmod(SLOTS * j, EIGHT)
            block = tiles[t]
            if start + SLOTS > EIGHT:
                block = jnp.where(place < start, tiles[t + 1], block)
            if start:
                block = pltpu.roll(block, EIGHT - start, 1)
            blocks.append(block.reshape(FLAT, HD).astype(bf16))
        wide = jnp.concatenate(blocks, axis=1)
        got = jnp.dot(hot, wide, preferred_element_type=f32)
        packed_ref[:, pair * 2 * HD : (pair + 1) * 2 * HD] = got.astype(bf16)
    same = row_ref[...] == col_ref[...]
    core = core_ref[0]
    for side, out_ref in enumerate((own_ref, other_ref)):
        first = 3 * (core if side == 0 else 1 - core)
        for i in range(3):

            def block_at(base):
                at = pl.multiple_of((first + i + base) * HD, HD)
                return packed_ref[:, pl.ds(at, HD)]

            prob = soft(block_at(0), block_at(HEADS_HERE), same).astype(bf16)
            value = block_at(2 * HEADS_HERE)
            out_ref[:, i * HD : (i + 1) * HD] = jnp.dot(
                prob, value, preferred_element_type=f32
            ).astype(bf16)


def grad_near_kernel(*refs):
    total = None
    for left, right in zip(refs[:6], refs[6:12]):
        product = jnp.dot(left[...], right[...], preferred_element_type=f32)
        total = product if total is None else total + product
    refs[12][...] = total


def grad_far_kernel(own_cot, other_cot, own_far, swap_far, near_ref, out_ref):
    total = near_ref[...] + jnp.dot(own_cot[...], own_far[...], preferred_element_type=f32)
    total = total + jnp.dot(other_cot[...], swap_far[...], preferred_element_type=f32)
    out_ref[...] = total.astype(bf16).reshape(out_ref.shape)


def gram_kernel(parts_ref, grad_ref, gram_ref):
    grad = jnp.sum(parts_ref[...].astype(f32), axis=0)
    grad_ref[...] = grad
    for h in range(3):
        head = grad[:, h * HD : (h + 1) * HD]
        gram_ref[h * HD : (h + 1) * HD, :] = lax.dot_general(
            head,
            head,
            (((0,), (0,)), ((), ())),
            precision=lax.Precision.HIGHEST,
            preferred_element_type=f32,
        )


def update_kernel(core_ref, gram_ref, grad_ref, here_ref, there_ref, hold_ref):
    def mul(a, b):
        return jnp.dot(a, b, precision=lax.Precision.HIGHEST, preferred_element_type=f32)

    row = lax.broadcasted_iota(jnp.int32, (HD, HD), 0)
    col = lax.broadcasted_iota(jnp.int32, (HD, HD), 1)
    eye = jnp.where(row == col, 1.0, 0.0).astype(f32)
    grams, norms = [], []
    for h in range(3):
        gram = gram_ref[h * HD : (h + 1) * HD, :]
        norm = jnp.sqrt(jnp.sum(gram * eye, axis=(0, 1), keepdims=True)) + norm_eps
        grams.append(gram / norm / norm)
        norms.append(norm)
    results = [None] * 3
    for step in range(NS_STEPS):
        squares = [mul(g, g) for g in grams]
        mixers = [
            coef_a * eye + coef_b * g + coef_c * s for g, s in zip(grams, squares)
        ]
        results = [m if r is None else mul(r, m) for r, m in zip(results, mixers)]
        if step + 1 < NS_STEPS:
            grams = [mul(g, m) for g, m in zip(grams, mixers)]
            grams = [mul(g, m) for g, m in zip(grams, mixers)]
    for h in range(3):
        field = grad_ref[:, h * HD : (h + 1) * HD] / norms[h]
        final = mul(field, results[h]) * math.sqrt(D)
        hold_ref[:, :, h * HD : (h + 1) * HD] = final.reshape(C, FEAT, HD)
    core = core_ref[0]
    here_ref[...] = hold_ref[core]
    there_ref[...] = hold_ref[1 - core]


def join_kernel(core_ref, here_ref, there_ref, out_ref):
    core = core_ref[0]
    out_ref[:, pl.ds(pl.multiple_of(core * HALF, HD), HALF)] = here_ref[...]
    out_ref[:, pl.ds(pl.multiple_of((1 - core) * HALF, HD), HALF)] = there_ref[...]


def backward_kernel(row_ref, col_ref, q_ref, k_ref, v_ref, d0, d1, d3, d2a, d2b, *refs):
    gq_ref, gk_ref, gv_ref = refs[-3:]
    same = row_ref[...] == col_ref[...]
    q, k, v = q_ref[...], k_ref[...], v_ref[...]
    d2 = jnp.concatenate([d2a[...], d2b[...]], axis=0)
    near = d0[...].astype(f32) + d1[...].astype(f32)
    d_out = (near + (d2.astype(f32) + d3[...].astype(f32))).astype(bf16)
    prob = soft(q, k, same)
    first = (((0,), (0,)), ((), ()))
    gv_ref[...] = lax.dot_general(
        prob.astype(bf16), d_out, first, preferred_element_type=f32
    ).astype(bf16)
    d_prob = lax.dot_general(d_out, v, (((1,), (1,)), ((), ())), preferred_element_type=f32)
    delta = jnp.sum(d_prob * prob, axis=-1, keepdims=True)
    d_score = (prob * (d_prob - delta) * scale).astype(bf16)
    gq_ref[...] = jnp.dot(d_score, k, preferred_element_type=f32).astype(bf16)
    gk_ref[...] = lax.dot_general(d_score, q, first, preferred_element_type=f32).astype(bf16)


def shift(field, axis, step):
    size = lax.axis_size(axis)
    return lax.ppermute(field, axis, [(i, (i + step) % size) for i in range(size)])


def cross(field, step):
    pairs = [(y * C + c, (y + step) % Y * C + 1 - c) for y in range(Y) for c in range(C)]
    return lax.ppermute(field, ("y", "c"), pairs)


def local(kernel, name, out_shape, *operands, scalars=0, far=0, room=24, **options):
    smem = pl.BlockSpec(memory_space=pltpu.SMEM)
    vmem = pl.BlockSpec(memory_space=pltpu.VMEM)
    hbm = pl.BlockSpec(memory_space=pltpu.HBM)
    return pl.pallas_call(
        kernel,
        in_specs=[smem] * scalars + [hbm] * far + [vmem] * (len(operands) - scalars - far),
        out_shape=out_shape,
        compiler_params=pltpu.CompilerParams(vmem_limit_bytes=room * 1024 * 1024),
        name=name,
        **options,
    )(*operands)


def array(shape, kind):
    return jax.ShapeDtypeStruct(shape, kind)


def shards(query, key, value, send_to, recv_from, segment, out_weight, cotangent):
    core = lax.axis_index("c")
    core_row = core.astype(jnp.int32).reshape(1)
    everything = ("z", "y", "c")

    field = pltpu.VMEM((ROWS, HEADS_HERE * HD), bf16)
    slots = local(
        place_kernel,
        "place",
        array((GROUPS, TILES * TILE, HD), bf16),
        query,
        key,
        value,
        send_to[None, :],
        far=3,
        room=60,
        scratch_shapes=[field, field, field, pltpu.SemaphoreType.DMA((3,))],
    )
    arrived = lax.all_to_all(slots, everything, split_axis=0, concat_axis=0, tiled=True)

    cotangent, slots = lax.optimization_barrier((cotangent, slots))
    feature = jnp.arange(X * FEAT * Y, dtype=jnp.int32).reshape(2, Y, C, FEAT)
    feature = feature.transpose(1, 0, 2, 3).reshape(Y, -1)
    feature = jnp.roll(feature, -lax.axis_index("y"), axis=0).reshape(-1)
    perm = (feature[:, None] == jnp.arange(feature.size)[None, :]).astype(bf16)
    turned = lax.dot_general(
        perm, cotangent, (((1,), (1,)), ((), ())), preferred_element_type=f32
    ).astype(bf16)
    turned = turned.reshape(Y, 4 * FEAT, ROWS)
    turned = [turned[0]] + [shift(turned[k], "y", k) for k in range(1, Y)]
    one, two = jnp.stack(turned[:2]), jnp.stack(turned[2:])
    one_up, two_down = shift(one, "x", 1), shift(two, "x", -1)
    two_up, one_down = shift(two, "x", 1), shift(one, "x", -1)
    one_far, two_far = shift(one_up, "x", 1), shift(two_down, "x", -1)
    cot_own = local(
        join_cot_kernel,
        "join_cot",
        array((Y, X * 4 * FEAT, ROWS), bf16),
        lax.axis_index("x").astype(jnp.int32).reshape(1),
        one,
        one_up,
        one_far,
        one_down,
        two,
        two_up,
        two_far,
        two_down,
        scalars=1,
        room=60,
    )
    cot_other = shift(cot_own, "c", 1)

    weight = lax.all_gather(out_weight, ("z", "c"), axis=0, tiled=True)
    part = array((ROWS, HEADS_HERE * HD), bf16)
    some = array((ROWS // 2, HEADS_HERE * HD), bf16)
    work = pl.CostEstimate(flops=18 * 10**9, bytes_accessed=54 * 10**6, transcendentals=0)
    d_parts = local(parts_kernel, "d_parts", (part,) * 3 + (some,) * 2, cot_own, weight, room=60, cost_estimate=work)
    arrived, cot_own, cot_other, *d_parts = lax.optimization_barrier(
        (arrived, cot_own, cot_other, *d_parts)
    )

    seg_row = segment[None, :]
    seg_col = segment[:, None]
    packed, own, other = local(
        forward_kernel,
        "forward",
        (
            array((ROWS, BLOCKS * HD), bf16),
            array((ROWS, HALF), bf16),
            array((ROWS, HALF), bf16),
        ),
        core_row,
        arrived,
        recv_from[None, :],
        recv_from[:, None],
        seg_row,
        seg_col,
        scalars=1,
    )

    own_up = shift(own, "y", 1)
    own_down = shift(own, "y", -1)
    swap = shift(other, "c", 1)
    swap_up = cross(other, 1)
    swap_down = cross(other, -1)
    own_far = shift(own_up, "y", 1)
    swap_far = shift(swap_down, "y", -1)
    grad = local(
        grad_near_kernel,
        "grad_near",
        array((Z * C * FEAT, HALF), f32),
        *[cot_own[k] for k in (0, 1, 3)],
        *[cot_other[k] for k in (0, 1, 3)],
        own,
        own_up,
        own_down,
        swap,
        swap_up,
        swap_down,
    )
    grad = local(
        grad_far_kernel,
        "grad_far",
        array((Z, C * FEAT, HALF), bf16),
        cot_own[2],
        cot_other[2],
        own_far,
        swap_far,
        grad,
    )
    grad, *d_parts = lax.optimization_barrier((grad, *d_parts))
    d_parts[3], d_parts[4] = shift(d_parts[3], "y", -1), shift(d_parts[4], "y", 1)
    d_parts[1], d_parts[2] = shift(d_parts[1], "y", -1), shift(d_parts[2], "y", 1)
    d_parts[3], d_parts[4] = shift(d_parts[3], "y", -1), shift(d_parts[4], "y", 1)
    parts = lax.all_to_all(grad, "z", split_axis=0, concat_axis=0, tiled=True)

    out = array((ROWS, HEADS_HERE * HD), bf16)

    def backward(heads, held):
        def column(base):
            return pl.BlockSpec((ROWS, HD), lambda h: (0, base + heads + h))

        return pl.pallas_call(
            backward_kernel,
            grid=(3,),
            in_specs=[
                pl.BlockSpec((1, ROWS), lambda h: (0, 0)),
                pl.BlockSpec((ROWS, 1), lambda h: (0, 0)),
                column(0),
                column(HEADS_HERE),
                column(2 * HEADS_HERE),
                *[column(0)] * 3,
                *[pl.BlockSpec((ROWS // 2, HD), lambda h: (0, heads + h))] * 2,
                *[pl.BlockSpec(memory_space=pl.ANY)] * len(held),
            ],
            out_specs=(column(0),) * 3,
            out_shape=(out,) * 3,
            input_output_aliases={10 + n: n for n in range(len(held))},
            compiler_params=pltpu.CompilerParams(vmem_limit_bytes=24 * 1024 * 1024),
            name="backward",
        )(seg_row, seg_col, packed, packed, packed, *d_parts, *held)

    grads = backward(0, ())

    grad, gram = local(
        gram_kernel,
        "gram",
        (array((C * FEAT, HALF), f32), array((3 * HD, HD), f32)),
        parts,
    )
    gram = gram.reshape(Z, -1, HD)
    gram = jnp.sum(lax.all_to_all(gram, "z", split_axis=0, concat_axis=0, tiled=True), axis=0)
    gram, *grads = lax.optimization_barrier((gram, *grads))
    gram = sum([shift(gram, "y", k) for k in range(1, Y)], gram)
    gram = jnp.broadcast_to(gram[None], (Z, *gram.shape))
    gram = lax.all_to_all(gram, "z", split_axis=0, concat_axis=0, tiled=True)
    grads = backward(3, grads)
    gram, *grads = lax.optimization_barrier((gram, *grads))
    half = array((FEAT, HALF), f32)
    here, there = local(
        update_kernel,
        "update",
        (half, half),
        core_row,
        gram.reshape(3 * HD, HD),
        grad,
        scalars=1,
        scratch_shapes=[pltpu.VMEM((C, FEAT, HALF), f32)],
    )
    there = shift(there, "c", 1)
    update = local(
        join_kernel, "join", array((FEAT, 2 * HALF), f32), core_row, here, there, scalars=1
    )

    return (*grads, update)


def solution(mesh):
    fine = Mesh(mesh.devices.reshape(Z, Y, C, X), ("z", "y", "c", "x"))
    everything = ("z", "y", "c")
    both = P(everything, "x")
    rows = P(everything)
    return jax.shard_map(
        shards,
        mesh=fine,
        in_specs=(both, both, both, rows, rows, rows, both, both),
        out_specs=(both, both, both, both),
        check_vma=False,
    )
```
